32 devices in a mesh: groups: 2 (over y), nodes: 16 (over z, x, core).
Axes of the slice: x: 2, y: 2, z: 4, core: 2. Of those that a mesh axis runs over, the one named last changes fastest.
Arguments:
- queries: bfloat16 [4096, 2048], P(('groups', 'nodes')), parts along dimension 0, may hold values from -192 to 192
- seg_kv: bfloat16 [2, 4096, 1024], P(None, ('groups', 'nodes')), parts along dimension 1, may hold values from -6 to 6
- kv_store: bfloat16 [2, 864, 128, 1024], P(None, ('groups', 'nodes')), parts along dimension 1, may hold values from -6 to 6
- seg_parent: int32 [8], P('groups'), parts along dimension 0, may hold values from 0 to 39, as said below
- block_up: int32 [80], P('groups'), parts along dimension 0, may hold values from -1 to 12, as said below
- page_owner: int32 [80, 4], P('groups'), parts along dimension 0, may hold values from 0 to 15, as said below
- page_slot: int32 [80, 4], P('groups'), parts along dimension 0, may hold values from 0 to 26, as said below
Outputs:
- attended: bfloat16 [4096, 2048], P(('groups', 'nodes')), parts along dimension 0
The draws below stay inside these ranges and needn't reach their ends.
There are 2 independent parts, one for each index of `groups`. The reference program is written for one: setup_inputs(seed, part) draws one part's arguments, and reference() takes and returns one part's arrays. A program takes and returns all parts, laid end to end along the dimension named above; each array names one. Nothing has to cross between parts.
Inputs may be any that keep to these rules, and one draw needn't show every extreme that they name: `block_up`: block 0 is the root and alone has -1; every other block's parent has a smaller number and lies one depth above it; depth d holds 3**d blocks, numbered in order of depth. `seg_parent`: some segment's parent is the last block, at depth 4 - 1, so that its path holds 4 blocks. `page_owner`: the pages of the blocks on one segment's path lie on distinct devices, so a device needs at most one page from each device, and some device needs one from every device; a device holds at most 27 pages, and some device holds 27. `page_slot`: no two pages share a device and a slot.
All inputs are finite; a program needn't handle non-finite values.
Results may differ from the reference program's by a relative error of at most 0.0035.
Values may be sent and summed in bfloat16 or wider, within the bound.
A program may use at most 64 MiB of HBM per device.

```python
import jax
import jax.numpy as jnp
import numpy as np
from jax import lax

HEADS = 16
KV_HEADS = 8
HEAD_DIM = 128
DEPTHS = 4
BRANCH = 3
BLOCK = 512
SEGS = 4
TOKENS = 2048
NBLK = 40
SLOTS = 27
PAGES = 4
PAGE_TOK = 128
N_NODES = 16


def tree_tables(key):
    key = jax.random.fold_in(key, 11)
    key_up, key_depth, key_pick, key_force, key_perm, key_rot, key_slot = jax.random.split(key, 7)
    level_size = np.array([BRANCH ** depth_step for depth_step in range(DEPTHS)], np.int32)
    level_start = np.array([(BRANCH ** depth_step - 1) // (BRANCH - 1) for depth_step in range(DEPTHS)], np.int32)
    block_depth = np.concatenate([np.full(BRANCH ** depth_step, depth_step, np.int32) for depth_step in range(DEPTHS)])
    level_place = np.concatenate([np.arange(BRANCH ** depth_step, dtype=np.int32) for depth_step in range(DEPTHS)])
    upper_depth = np.maximum(block_depth - 1, 0)
    last_in_level = level_place == level_size[block_depth] - 1
    raw_up = jax.random.randint(key_up, (NBLK,), 0, 1 << 30)
    block_up = jnp.asarray(level_start[upper_depth]) + raw_up % jnp.asarray(level_size[upper_depth])
    block_up = jnp.where(jnp.asarray(last_in_level), jnp.asarray(level_start[block_depth] - 1), block_up)
    block_up = jnp.where(jnp.asarray(block_depth) > 0, block_up, -1).astype(jnp.int32)
    seg_depth = jax.random.randint(key_depth, (SEGS,), 0, DEPTHS)
    forced = jax.random.randint(key_force, (), 0, SEGS)
    raw_pick = jax.random.randint(key_pick, (SEGS,), 0, 1 << 30)
    seg_parent = jnp.asarray(level_start)[seg_depth] + raw_pick % jnp.asarray(level_size)[seg_depth]
    seg_parent = jnp.where(jnp.arange(SEGS) == forced, NBLK - 1, seg_parent)
    shuffle = jax.random.permutation(key_perm, N_NODES).astype(jnp.int32)
    rotation = jax.random.randint(key_rot, (NBLK, 1), 0, PAGES)
    band_place = jnp.asarray(block_depth)[:, None] * PAGES + (jnp.arange(PAGES)[None, :] + rotation) % PAGES
    page_owner = shuffle[band_place]
    slot_keys = jax.random.split(key_slot, N_NODES)
    owner_order = jax.vmap(lambda one_key: jax.random.permutation(one_key, SLOTS))(slot_keys)
    page_slot = owner_order[page_owner, jnp.asarray(level_place)[:, None]]
    return (seg_parent.astype(jnp.int32), block_up, page_owner.astype(jnp.int32), page_slot.astype(jnp.int32))


def attention_inputs(key):
    key = jax.random.fold_in(key, 29)
    key_query, key_pair = jax.random.split(key, 2)
    kv_width = KV_HEADS * HEAD_DIM
    queries = 2.0 * jax.random.normal(key_query, (TOKENS, HEADS * HEAD_DIM), jnp.float32)
    kv_pairs = jax.random.normal(key_pair, (2, TOKENS, kv_width), jnp.float32)
    queries = jnp.clip(queries, -192.0, 192.0).astype(jnp.bfloat16)
    kv_pairs = jnp.clip(kv_pairs, -6.0, 6.0).astype(jnp.bfloat16)
    return (queries, kv_pairs)


def draw_queries(key, part):
    return attention_inputs(key)[0]


def draw_seg_kv(key, part):
    return attention_inputs(key)[1]


def draw_seg_parent(key, part):
    return tree_tables(key)[0]


def draw_block_up(key, part):
    return tree_tables(key)[1]


def draw_page_owner(key, part):
    return tree_tables(key)[2]


def draw_page_slot(key, part):
    return tree_tables(key)[3]


def level_of(rng, dims, shards, least, high):
    def one(axis_at, parts):
        heights = jax.random.uniform(jax.random.fold_in(jax.random.fold_in(rng, 6), axis_at), (parts,), jnp.float32, least / len(shards), high / len(shards))
        return jnp.repeat(jnp.exp(heights), dims[axis_at] // parts).reshape((-1,) + (1,) * (len(dims) - axis_at - 1))

    gain = one(*shards[0])
    for cut in shards[1:]:
        gain = gain * one(*cut)
    return gain


def normal_values(own_key, extent, spread, most, shards=(), kind=jnp.bfloat16):
    loudness = level_of(own_key, extent, shards, -0.22, 0.18) if shards else 1.0
    entries = jax.random.normal(own_key, extent, jnp.float32) * spread * loudness
    return jnp.minimum(jnp.maximum(entries, -most), most).astype(kind)


def setup_inputs(seed: int = 0, part: int = 0) -> dict:
    arg_keys = jax.random.split(jax.random.key(seed), 8)
    own_keys = jax.random.split(jax.random.fold_in(arg_keys[7], part), 8)
    queries = draw_queries(jax.random.fold_in(jax.random.fold_in(arg_keys[7], part), 71), part)
    seg_kv = draw_seg_kv(jax.random.fold_in(jax.random.fold_in(arg_keys[7], part), 71), part)
    kv_store = normal_values(own_keys[2], (2, N_NODES * SLOTS, PAGE_TOK, KV_HEADS * HEAD_DIM), 1.0, 6.0, ((1, 16),))
    seg_parent = draw_seg_parent(jax.random.fold_in(jax.random.fold_in(arg_keys[7], part), 71), part)
    block_up = draw_block_up(jax.random.fold_in(jax.random.fold_in(arg_keys[7], part), 71), part)
    page_owner = draw_page_owner(jax.random.fold_in(jax.random.fold_in(arg_keys[7], part), 71), part)
    page_slot = draw_page_slot(jax.random.fold_in(jax.random.fold_in(arg_keys[7], part), 71), part)
    return dict(queries=queries, seg_kv=seg_kv, kv_store=kv_store, seg_parent=seg_parent, block_up=block_up, page_owner=page_owner, page_slot=page_slot)


query_scale = 168.0 ** -0.5


def walk_paths(seg_parent, block_up):
    chain_list = []
    current = seg_parent
    for depth_step in range(DEPTHS):
        chain_list.append(current)
        safe_blocks = jnp.maximum(current, 0).astype(jnp.int32)
        current = jnp.where(current >= 0, block_up[safe_blocks], -1).astype(jnp.int32)
    return jnp.stack(chain_list, axis=1)


def reference(queries, seg_kv, kv_store, seg_parent, block_up, page_owner, page_slot):
    path_blocks = walk_paths(seg_parent, block_up)
    head_group = HEADS // KV_HEADS
    kv_width = KV_HEADS * HEAD_DIM
    positions = jnp.arange(BLOCK)
    own_live = positions[None, :] <= positions[:, None]

    def one_segment(segment):
        blocks = path_blocks[segment]
        path_live = blocks >= 0
        safe_blocks = jnp.maximum(blocks, 0).astype(jnp.int32)
        store_rows = (page_owner[safe_blocks] * SLOTS + page_slot[safe_blocks]).reshape(-1).astype(jnp.int32)
        ancestors = jnp.take(kv_store, store_rows, axis=1).reshape(2, DEPTHS * BLOCK, kv_width)
        anc_live = jnp.repeat(path_live, BLOCK)
        row_start = (segment * BLOCK).astype(jnp.int32)
        own_kv = lax.dynamic_slice_in_dim(seg_kv, row_start, BLOCK, 1)
        all_kv = jnp.concatenate([own_kv, ancestors], axis=1).astype(jnp.float32)
        visible = jnp.concatenate([own_live, jnp.broadcast_to(anc_live[None, :], (BLOCK, DEPTHS * BLOCK))], axis=1)
        query_rows = lax.dynamic_slice_in_dim(queries, row_start, BLOCK, 0).astype(jnp.float32)
        query_rows = query_rows.reshape(BLOCK, KV_HEADS, head_group, HEAD_DIM)
        key_rows = all_kv[0].reshape(-1, KV_HEADS, HEAD_DIM)
        value_rows = all_kv[1].reshape(-1, KV_HEADS, HEAD_DIM)
        scores = jnp.einsum("tkgd,nkd->tkgn", query_rows, key_rows) * query_scale
        scores = jnp.where(visible[:, None, None, :], scores, -jnp.inf)
        row_max = jnp.max(scores, axis=-1, keepdims=True)
        weights = jnp.exp(scores - row_max)
        weight_sum = jnp.sum(weights, axis=-1)
        rounded = lax.optimization_barrier(weights.astype(jnp.bfloat16)).astype(jnp.float32)
        mixed_sum = jnp.einsum("tkgn,nkd->tkgd", rounded, value_rows)
        return (mixed_sum / weight_sum[..., None]).astype(jnp.bfloat16).reshape(BLOCK, HEADS * HEAD_DIM)

    result = lax.map(one_segment, jnp.arange(N_NODES // 4, dtype=jnp.int32))
    return result.reshape(TOKENS, HEADS * HEAD_DIM)
```

```python
import functools
import math

import jax
import jax.numpy as jnp
from jax import lax
from jax.experimental import pallas as pl
from jax.experimental.pallas import tpu as pltpu
from jax.sharding import PartitionSpec as P

HEADS = 16
KV_HEADS = 8
HEAD_DIM = 128
DEPTHS = 4
TEAM = 4

score_scale = 168.0 ** (-0.5)
log2_scale = score_scale * math.log2(math.e)
DEAD = -1e30


def pick_kernel(up_ref, parent_ref, owner_ref, slot_ref, store_ref, out_ref, live_ref, sems):
    me = lax.axis_index("nodes")
    my_segment = me // TEAM
    nodes = out_ref.shape[0]
    segs = nodes // TEAM
    pages = owner_ref.shape[1]
    width = out_ref.shape[3]

    def clear(node, carry):
        live_ref[node] = jnp.float32(DEAD)
        return carry

    lax.fori_loop(0, nodes, clear, 0)

    def copies(seg, slot):
        return [
            pltpu.make_async_copy(
                store_ref.at[:, slot, :, part * width : (part + 1) * width],
                out_ref.at[seg * TEAM + part],
                sems.at[seg * TEAM + part],
            )
            for part in range(TEAM)
        ]

    def one_segment(seg, carry):
        current = parent_ref[seg]
        slot = jnp.int32(0)
        for _ in range(DEPTHS):
            live = current >= 0
            safe = jnp.maximum(current, 0)

            def one_page(page, slot):
                owner = owner_ref[safe, page]
                hit = jnp.logical_and(live, owner == me)

                @pl.when(jnp.logical_and(live, seg == my_segment))
                def _():
                    live_ref[owner] = jnp.float32(0)

                return jnp.where(hit, slot_ref[safe, page], slot)

            slot = lax.fori_loop(0, pages, one_page, slot, unroll=pages <= 4)
            current = jnp.where(live, up_ref[safe], -1)
        for copy in copies(seg, slot):
            copy.start()
        return carry

    lax.fori_loop(0, segs, one_segment, 0)

    def finish(seg, carry):
        for copy in copies(seg, 0):
            copy.wait()
        return carry

    lax.fori_loop(0, segs, finish, 0)


def attend_kernel(
    live_ref, q_ref, kv_ref, page_ref, out_ref,
    q_buf, own_buf, anc_buf, acc_ref, max_ref, sum_ref, res_buf,
    q_send, q_recv, kv_send, kv_recv, page_send, page_recv, res_send, res_recv,
):
    me = lax.axis_index("nodes")
    member = me % TEAM
    segment = me // TEAM
    nodes = page_ref.shape[0]
    segs = nodes // TEAM
    tok = q_ref.shape[0]
    seg_tok = tok * TEAM
    q_cols = q_buf.shape[2]
    kv_cols = own_buf.shape[3]
    page_tok = page_ref.shape[2]
    heads = q_cols // HEAD_DIM
    group = HEADS // KV_HEADS

    barrier = pltpu.get_barrier_semaphore()

    def greet(step, carry):
        other = lax.rem(me + step, nodes)
        pl.semaphore_signal(barrier, inc=1, device_id={"nodes": other}, device_id_type=pl.DeviceIdType.MESH)
        return carry

    lax.fori_loop(1, nodes, greet, 0)
    pl.semaphore_wait(barrier, nodes - 1)

    def q_copy(step):
        peer = lax.rem(member + step, TEAM)
        return pltpu.make_async_remote_copy(
            src_ref=q_ref.at[:, pl.ds(pl.multiple_of(peer * q_cols, q_cols), q_cols)],
            dst_ref=q_buf.at[member],
            send_sem=q_send.at[peer],
            recv_sem=q_recv.at[member],
            device_id={"nodes": segment * TEAM + peer},
            device_id_type=pl.DeviceIdType.MESH,
        )

    def kv_copy(step):
        peer = lax.rem(member + step, TEAM)
        return pltpu.make_async_remote_copy(
            src_ref=kv_ref.at[:, :, pl.ds(pl.multiple_of(peer * kv_cols, kv_cols), kv_cols)],
            dst_ref=own_buf.at[:, member],
            send_sem=kv_send.at[peer],
            recv_sem=kv_recv.at[member],
            device_id={"nodes": segment * TEAM + peer},
            device_id_type=pl.DeviceIdType.MESH,
        )

    def q_local():
        return pltpu.make_async_copy(
            q_ref.at[:, pl.ds(pl.multiple_of(member * q_cols, q_cols), q_cols)], q_buf.at[member], q_recv.at[member]
        )

    def kv_local():
        return pltpu.make_async_copy(
            kv_ref.at[:, :, pl.ds(pl.multiple_of(member * kv_cols, kv_cols), kv_cols)],
            own_buf.at[:, member],
            kv_recv.at[member],
        )

    def page_copy(dest):
        return pltpu.make_async_remote_copy(
            src_ref=page_ref.at[dest],
            dst_ref=anc_buf.at[:, me],
            send_sem=page_send.at[dest],
            recv_sem=page_recv.at[me],
            device_id={"nodes": dest},
            device_id_type=pl.DeviceIdType.MESH,
        )

    def page_local():
        return pltpu.make_async_copy(page_ref.at[me], anc_buf.at[:, me], page_recv.at[me])

    low = segment < segs // 2

    def far_segment(step):
        return jnp.where(low, segs - 1 - step, step)

    for step in range(1, TEAM):
        q_copy(step).start()
        kv_copy(step).start()
    q_local().start()
    kv_local().start()
    page_local().start()

    def send_pages(index, carry):
        seg = far_segment(index // TEAM)
        dest = seg * TEAM + lax.rem(member + index, TEAM)

        @pl.when(dest != me)
        def _():
            page_copy(dest).start()

        return carry

    lax.fori_loop(0, nodes, send_pages, 0)

    for step in range(TEAM):
        peer = lax.rem(member + step, TEAM)
        pltpu.make_async_copy(q_buf.at[peer], q_buf.at[peer], q_recv.at[peer]).wait()
        pltpu.make_async_copy(own_buf.at[:, peer], own_buf.at[:, peer], kv_recv.at[peer]).wait()

    def head_query(head):
        cols = pl.ds(pl.multiple_of(head * HEAD_DIM, HEAD_DIM), HEAD_DIM)
        return q_buf[:, :, cols].reshape(seg_tok, HEAD_DIM)

    def kv_columns(head):
        return pl.ds(pl.multiple_of(head // group * HEAD_DIM, HEAD_DIM), HEAD_DIM)

    def own_head(head):
        cols = kv_columns(head)
        keys = own_buf[0, :, :, cols].reshape(seg_tok, HEAD_DIM)
        values = own_buf[1, :, :, cols].reshape(seg_tok, HEAD_DIM)
        scores = lax.dot_general(
            head_query(head), keys, (((1,), (1,)), ((), ())), preferred_element_type=jnp.float32
        )
        rows = lax.broadcasted_iota(jnp.int32, scores.shape, 0)
        columns = lax.broadcasted_iota(jnp.int32, scores.shape, 1)
        scores = jnp.where(columns <= rows, scores, DEAD)
        row_max = jnp.max(scores, axis=-1, keepdims=True)
        weights = jnp.exp2((scores - row_max) * log2_scale)
        max_ref[head] = row_max
        sum_ref[head] = jnp.sum(weights, axis=-1, keepdims=True)
        acc_ref[head] = jnp.dot(weights.astype(jnp.bfloat16), values, preferred_element_type=jnp.float32)

    pl.loop(0, heads)(own_head)

    def one_step(step, carry):
        seg = far_segment(step)
        first = pl.multiple_of(seg * TEAM, TEAM)
        for part in range(TEAM):
            block = anc_buf.at[:, first + part]
            pltpu.make_async_copy(block, block, page_recv.at[first + part]).wait()
        bias = jnp.concatenate(
            [jnp.full((1, page_tok), live_ref[first + part], jnp.float32) for part in range(TEAM)], axis=1
        )

        def one_head(head):
            cols = kv_columns(head)
            keys = anc_buf[0, pl.ds(first, TEAM), :, cols].reshape(TEAM * page_tok, HEAD_DIM)
            values = anc_buf[1, pl.ds(first, TEAM), :, cols].reshape(TEAM * page_tok, HEAD_DIM)
            scores = lax.dot_general(
                head_query(head), keys, (((1,), (1,)), ((), ())), preferred_element_type=jnp.float32
            )
            scores = scores + bias
            old_max = max_ref[head]
            new_max = jnp.maximum(old_max, jnp.max(scores, axis=-1, keepdims=True))
            weights = jnp.exp2((scores - new_max) * log2_scale)
            shrink = jnp.exp2((old_max - new_max) * log2_scale)
            max_ref[head] = new_max
            sum_ref[head] = sum_ref[head] * shrink + jnp.sum(weights, axis=-1, keepdims=True)
            acc_ref[head] = acc_ref[head] * shrink + jnp.dot(
                weights.astype(jnp.bfloat16), values, preferred_element_type=jnp.float32
            )

        pl.loop(0, heads)(one_head)
        return carry

    lax.fori_loop(0, segs, one_step, 0)

    def res_copy(step, half):
        peer = lax.rem(member + step, TEAM)
        columns = q_cols // 2
        return pltpu.make_async_remote_copy(
            src_ref=res_buf.at[half, peer],
            dst_ref=out_ref.at[:, pl.ds(pl.multiple_of(member * q_cols + half * columns, columns), columns)],
            send_sem=res_send.at[half, peer],
            recv_sem=res_recv.at[half, member],
            device_id={"nodes": segment * TEAM + peer},
            device_id_type=pl.DeviceIdType.MESH,
        )

    def res_local(half):
        columns = q_cols // 2
        return pltpu.make_async_copy(
            res_buf.at[half, member],
            out_ref.at[:, pl.ds(pl.multiple_of(member * q_cols + half * columns, columns), columns)],
            res_recv.at[half, member],
        )

    half_heads = heads // 2
    for half in range(2):
        for place in range(half_heads):
            head = half * half_heads + place
            result = (acc_ref[head] / sum_ref[head]).astype(jnp.bfloat16)
            res_buf[half, :, :, place * HEAD_DIM : (place + 1) * HEAD_DIM] = result.reshape(TEAM, tok, HEAD_DIM)
        for step in range(1, TEAM):
            res_copy(step, half).start()
        res_local(half).start()

    columns = q_cols // 2
    for half in range(2):
        for step in range(TEAM):
            peer = lax.rem(member + step, TEAM)
            place = out_ref.at[:, pl.ds(pl.multiple_of(peer * q_cols + half * columns, columns), columns)]
            pltpu.make_async_copy(place, place, res_recv.at[half, peer]).wait()
        for step in range(1, TEAM):
            res_copy(step, half).wait_send()
    for step in range(1, TEAM):
        q_copy(step).wait_send()
        kv_copy(step).wait_send()

    def drain(step, carry):
        page_copy(lax.rem(me + step, nodes)).wait_send()
        return carry

    lax.fori_loop(1, nodes, drain, 0)


def local(queries, seg_kv, kv_store, seg_parent, block_up, page_owner, page_slot):
    nodes = lax.axis_size("nodes")
    tok, q_width = queries.shape
    kv_width = seg_kv.shape[2]
    page_tok = kv_store.shape[2]
    q_cols = q_width // TEAM
    kv_cols = kv_width // TEAM
    heads = q_cols // HEAD_DIM
    smem = pl.BlockSpec(memory_space=pltpu.SMEM)
    anywhere = pl.BlockSpec(memory_space=pl.ANY)
    outgoing, live = pl.pallas_call(
        pick_kernel,
        out_shape=(
            jax.ShapeDtypeStruct((nodes, 2, page_tok, kv_cols), kv_store.dtype),
            jax.ShapeDtypeStruct((nodes,), jnp.float32),
        ),
        in_specs=[smem, smem, smem, smem, anywhere],
        out_specs=(anywhere, smem),
        scratch_shapes=[pltpu.SemaphoreType.DMA((nodes,))],
        name="pick_pages",
    )(block_up, seg_parent, page_owner, page_slot, kv_store)
    dma = pltpu.SemaphoreType.DMA
    return pl.pallas_call(
        attend_kernel,
        out_shape=jax.ShapeDtypeStruct((tok, q_width), jnp.bfloat16),
        in_specs=[smem, anywhere, anywhere, anywhere],
        out_specs=anywhere,
        scratch_shapes=[
            pltpu.VMEM((TEAM, tok, q_cols), jnp.bfloat16),
            pltpu.VMEM((2, TEAM, tok, kv_cols), jnp.bfloat16),
            pltpu.VMEM((2, nodes, page_tok, kv_cols), jnp.bfloat16),
            pltpu.VMEM((heads, TEAM * tok, HEAD_DIM), jnp.float32),
            pltpu.VMEM((heads, TEAM * tok, 1), jnp.float32),
            pltpu.VMEM((heads, TEAM * tok, 1), jnp.float32),
            pltpu.VMEM((2, TEAM, tok, q_cols // 2), jnp.bfloat16),
            dma((TEAM,)), dma((TEAM,)), dma((TEAM,)), dma((TEAM,)),
            dma((nodes,)), dma((nodes,)), dma((2, TEAM)), dma((2, TEAM)),
        ],
        compiler_params=pltpu.CompilerParams(
            collective_id=0, has_side_effects=True, vmem_limit_bytes=40 * 1024 * 1024
        ),
        name="tree_attention",
    )(live, queries, seg_kv, outgoing)


def solution(mesh):
    in_specs = (
        P(("groups", "nodes"), None),
        P(None, ("groups", "nodes"), None),
        P(None, ("groups", "nodes"), None, None),
        P("groups"),
        P("groups"),
        P("groups", None),
        P("groups", None),
    )
    out_specs = P(("groups", "nodes"), None)
    return jax.shard_map(local, mesh=mesh, in_specs=in_specs, out_specs=out_specs, check_vma=False)
```

```python
import functools
import math

import jax
import jax.numpy as jnp
from jax import lax
from jax.experimental import pallas as pl
from jax.experimental.pallas import tpu as pltpu
from jax.sharding import PartitionSpec as P

HEADS = 16
KV_HEADS = 8
HEAD_DIM = 128
DEPTHS = 4
TEAM = 4

score_scale = 168.0 ** (-0.5)
log2_scale = score_scale * math.log2(math.e)
DEAD = -1e30


def pick_kernel(up_ref, parent_ref, owner_ref, slot_ref, store_ref, out_ref, live_ref, sems):
    me = lax.axis_index("nodes")
    my_segment = me // TEAM
    nodes = live_ref.shape[0]
    segs = out_ref.shape[1]
    pages = owner_ref.shape[0]

    def clear(node, carry):
        live_ref[node] = jnp.float32(DEAD)
        return carry

    lax.fori_loop(0, nodes, clear, 0)

    def copies(seg, slot):
        return [
            pltpu.make_async_copy(store_ref.at[half, slot], out_ref.at[half, seg], sems.at[half, seg])
            for half in range(2)
        ]

    def one_segment(seg, carry):
        current = parent_ref[seg]
        slot = jnp.int32(0)
        for _ in range(DEPTHS):
            live = current >= 0
            safe = jnp.maximum(current, 0)

            def one_page(page, slot):
                owner = owner_ref[page, safe]
                hit = jnp.logical_and(live, owner == me)

                @pl.when(jnp.logical_and(live, seg == my_segment))
                def _():
                    live_ref[owner] = jnp.float32(0)

                return jnp.where(hit, slot_ref[page, safe], slot)

            slot = lax.fori_loop(0, pages, one_page, slot, unroll=pages <= 4)
            current = jnp.where(live, up_ref[safe], -1)
        for copy in copies(seg, slot):
            copy.start()
        return carry

    lax.fori_loop(0, segs, one_segment, 0)

    def finish(seg, carry):
        for copy in copies(seg, 0):
            copy.wait()
        return carry

    lax.fori_loop(0, segs, finish, 0)


def attend_kernel(
    live_ref, q_ref, kv_ref, page_ref, out_ref,
    q_buf, own_buf, anc_buf, acc_ref, max_ref, sum_ref, res_buf,
    q_send, q_recv, kv_send, kv_recv, page_send, page_recv, res_send, res_recv,
):
    me = lax.axis_index("nodes")
    member = me % TEAM
    segment = me // TEAM
    segs = page_ref.shape[1]
    nodes = segs * TEAM
    tok = q_ref.shape[0]
    seg_tok = tok * TEAM
    q_cols = q_buf.shape[2]
    kv_cols = own_buf.shape[3]
    page_tok = page_ref.shape[2]
    heads = q_cols // HEAD_DIM
    group = HEADS // KV_HEADS

    barrier = pltpu.get_barrier_semaphore()

    def greet(step, carry):
        other = lax.rem(me + step, nodes)
        pl.semaphore_signal(barrier, inc=1, device_id={"nodes": other}, device_id_type=pl.DeviceIdType.MESH)
        return carry

    lax.fori_loop(1, nodes, greet, 0)
    pl.semaphore_wait(barrier, nodes - 1)

    def q_copy(step):
        peer = lax.rem(member + step, TEAM)
        return pltpu.make_async_remote_copy(
            src_ref=q_ref.at[:, pl.ds(pl.multiple_of(peer * q_cols, q_cols), q_cols)],
            dst_ref=q_buf.at[member],
            send_sem=q_send.at[peer],
            recv_sem=q_recv.at[member],
            device_id={"nodes": segment * TEAM + peer},
            device_id_type=pl.DeviceIdType.MESH,
        )

    def kv_copy(step):
        peer = lax.rem(member + step, TEAM)
        return pltpu.make_async_remote_copy(
            src_ref=kv_ref.at[:, :, pl.ds(pl.multiple_of(peer * kv_cols, kv_cols), kv_cols)],
            dst_ref=own_buf.at[:, member],
            send_sem=kv_send.at[peer],
            recv_sem=kv_recv.at[member],
            device_id={"nodes": segment * TEAM + peer},
            device_id_type=pl.DeviceIdType.MESH,
        )

    def q_local():
        return pltpu.make_async_copy(
            q_ref.at[:, pl.ds(pl.multiple_of(member * q_cols, q_cols), q_cols)], q_buf.at[member], q_recv.at[member]
        )

    def kv_local():
        return pltpu.make_async_copy(
            kv_ref.at[:, :, pl.ds(pl.multiple_of(member * kv_cols, kv_cols), kv_cols)],
            own_buf.at[:, member],
            kv_recv.at[member],
        )

    def page_part(dest):
        start = lax.rem(dest, TEAM) * kv_cols
        return page_ref.at[:, dest // TEAM, :, pl.ds(pl.multiple_of(start, kv_cols), kv_cols)]

    def page_copy(dest):
        return pltpu.make_async_remote_copy(
            src_ref=page_part(dest),
            dst_ref=anc_buf.at[:, me],
            send_sem=page_send.at[dest],
            recv_sem=page_recv.at[me],
            device_id={"nodes": dest},
            device_id_type=pl.DeviceIdType.MESH,
        )

    def page_local():
        return pltpu.make_async_copy(page_part(me), anc_buf.at[:, me], page_recv.at[me])

    low = segment < segs // 2

    def far_segment(step):
        return jnp.where(low, segs - 1 - step, step)

    for step in range(1, TEAM):
        q_copy(step).start()
        kv_copy(step).start()
    q_local().start()
    kv_local().start()
    page_local().start()

    def send_pages(index, carry):
        seg = far_segment(index // TEAM)
        dest = seg * TEAM + lax.rem(member + index, TEAM)

        @pl.when(dest != me)
        def _():
            page_copy(dest).start()

        return carry

    lax.fori_loop(0, nodes, send_pages, 0)

    for step in range(TEAM):
        peer = lax.rem(member + step, TEAM)
        pltpu.make_async_copy(q_buf.at[peer], q_buf.at[peer], q_recv.at[peer]).wait()
        pltpu.make_async_copy(own_buf.at[:, peer], own_buf.at[:, peer], kv_recv.at[peer]).wait()

    def head_query(head):
        cols = pl.ds(head * HEAD_DIM, HEAD_DIM)
        return q_buf[:, :, cols].reshape(seg_tok, HEAD_DIM)

    def kv_columns(head):
        return pl.ds(head // group * HEAD_DIM, HEAD_DIM)

    def weighted(values, weights):
        return lax.dot_general(
            values, weights.astype(jnp.bfloat16), (((0,), (0,)), ((), ())), preferred_element_type=jnp.float32
        )

    def score(keys, head):
        return lax.dot_general(
            keys, head_query(head), (((1,), (1,)), ((), ())), preferred_element_type=jnp.float32
        )

    def own_head(head):
        cols = kv_columns(head)
        keys = own_buf[0, :, :, cols].reshape(seg_tok, HEAD_DIM)
        values = own_buf[1, :, :, cols].reshape(seg_tok, HEAD_DIM)
        scores = score(keys, head)
        key_at = lax.broadcasted_iota(jnp.int32, scores.shape, 0)
        query_at = lax.broadcasted_iota(jnp.int32, scores.shape, 1)
        scores = jnp.where(key_at <= query_at, scores, DEAD)
        row_max = jnp.max(scores, axis=0, keepdims=True)
        weights = jnp.exp2((scores - row_max) * log2_scale)
        max_ref[head] = row_max
        sum_ref[head] = jnp.sum(weights, axis=0, keepdims=True)
        acc_ref[head] = weighted(values, weights)

    for head in range(heads):
        own_head(head)

    def res_copy(step, half):
        peer = lax.rem(member + step, TEAM)
        columns = q_cols // 2
        return pltpu.make_async_remote_copy(
            src_ref=res_buf.at[half, peer],
            dst_ref=out_ref.at[:, pl.ds(pl.multiple_of(member * q_cols + half * columns, columns), columns)],
            send_sem=res_send.at[half, peer],
            recv_sem=res_recv.at[half, member],
            device_id={"nodes": segment * TEAM + peer},
            device_id_type=pl.DeviceIdType.MESH,
        )

    def res_local(half):
        columns = q_cols // 2
        return pltpu.make_async_copy(
            res_buf.at[half, member],
            out_ref.at[:, pl.ds(pl.multiple_of(member * q_cols + half * columns, columns), columns)],
            res_recv.at[half, member],
        )

    half_heads = heads // 2

    def give(half):
        for place in range(half_heads):
            head = half * half_heads + place
            result = (acc_ref[head] / sum_ref[head]).T.astype(jnp.bfloat16)
            res_buf[half, :, :, place * HEAD_DIM : (place + 1) * HEAD_DIM] = result.reshape(TEAM, tok, HEAD_DIM)
        for step in range(1, TEAM):
            res_copy(step, half).start()
        res_local(half).start()

    def one_step(step, last):
        seg = far_segment(segs - 1 - step)
        first = pl.multiple_of(seg * TEAM, TEAM)
        for part in range(TEAM):
            block = anc_buf.at[:, first + part]
            pltpu.make_async_copy(block, block, page_recv.at[first + part]).wait()
        def one_head(head):
            cols = kv_columns(head)
            keys = anc_buf[0, pl.ds(first, TEAM), :, cols].reshape(TEAM * page_tok, HEAD_DIM)
            values = anc_buf[1, pl.ds(first, TEAM), :, cols].reshape(TEAM * page_tok, HEAD_DIM)
            scores = score(keys, head)
            scores = jnp.concatenate(
                [
                    scores[part * page_tok : (part + 1) * page_tok] + live_ref[first + part]
                    for part in range(TEAM)
                ],
                axis=0,
            )
            old_max = max_ref[head]
            new_max = jnp.maximum(old_max, jnp.max(scores, axis=0, keepdims=True))
            weights = jnp.exp2((scores - new_max) * log2_scale)
            shrink = jnp.exp2((old_max - new_max) * log2_scale)
            max_ref[head] = new_max
            sum_ref[head] = sum_ref[head] * shrink + jnp.sum(weights, axis=0, keepdims=True)
            acc_ref[head] = acc_ref[head] * shrink + weighted(values, weights)

        for head in range(heads):
            one_head(head)
            if last and head % half_heads == half_heads - 1:
                give(head // half_heads)

    def early_step(step, carry):
        one_step(step, False)
        return carry

    lax.fori_loop(0, segs - 1, early_step, 0)
    one_step(segs - 1, True)

    columns = q_cols // 2
    for half in range(2):
        for step in range(TEAM):
            peer = lax.rem(member + step, TEAM)
            place = out_ref.at[:, pl.ds(pl.multiple_of(peer * q_cols + half * columns, columns), columns)]
            pltpu.make_async_copy(place, place, res_recv.at[half, peer]).wait()
        for step in range(1, TEAM):
            res_copy(step, half).wait_send()
    for step in range(1, TEAM):
        q_copy(step).wait_send()
        kv_copy(step).wait_send()

    def drain(step, carry):
        page_copy(lax.rem(me + step, nodes)).wait_send()
        return carry

    lax.fori_loop(1, nodes, drain, 0)


def local(queries, seg_kv, kv_store, seg_parent, block_up, page_owner, page_slot):
    nodes = lax.axis_size("nodes")
    tok, q_width = queries.shape
    kv_width = seg_kv.shape[2]
    page_tok = kv_store.shape[2]
    q_cols = q_width // TEAM
    kv_cols = kv_width // TEAM
    heads = q_cols // HEAD_DIM
    smem = pl.BlockSpec(memory_space=pltpu.SMEM)
    anywhere = pl.BlockSpec(memory_space=pl.ANY)
    outgoing, live = pl.pallas_call(
        pick_kernel,
        out_shape=(
            pltpu.VMEM((2, nodes // TEAM, page_tok, kv_width), kv_store.dtype),
            jax.ShapeDtypeStruct((nodes,), jnp.float32),
        ),
        in_specs=[smem, smem, smem, smem, pl.BlockSpec(memory_space=pltpu.HBM)],
        out_specs=(pl.BlockSpec(memory_space=pltpu.VMEM), smem),
        scratch_shapes=[pltpu.SemaphoreType.DMA((2, nodes // TEAM))],
        compiler_params=pltpu.CompilerParams(vmem_limit_bytes=52 * 1024 * 1024),
        name="pick_pages",
    )(block_up, seg_parent, page_owner.T, page_slot.T, kv_store)
    dma = pltpu.SemaphoreType.DMA
    return pl.pallas_call(
        attend_kernel,
        out_shape=jax.ShapeDtypeStruct((tok, q_width), jnp.bfloat16),
        in_specs=[smem, anywhere, anywhere, anywhere],
        out_specs=anywhere,
        scratch_shapes=[
            pltpu.VMEM((TEAM, tok, q_cols), jnp.bfloat16),
            pltpu.VMEM((2, TEAM, tok, kv_cols), jnp.bfloat16),
            pltpu.VMEM((2, nodes, page_tok, kv_cols), jnp.bfloat16),
            pltpu.VMEM((heads, HEAD_DIM, TEAM * tok), jnp.float32),
            pltpu.VMEM((heads, 1, TEAM * tok), jnp.float32),
            pltpu.VMEM((heads, 1, TEAM * tok), jnp.float32),
            pltpu.VMEM((2, TEAM, tok, q_cols // 2), jnp.bfloat16),
            dma((TEAM,)), dma((TEAM,)), dma((TEAM,)), dma((TEAM,)),
            dma((nodes,)), dma((nodes,)), dma((2, TEAM)), dma((2, TEAM)),
        ],
        compiler_params=pltpu.CompilerParams(
            collective_id=0, has_side_effects=True, vmem_limit_bytes=40 * 1024 * 1024
        ),
        name="tree_attention",
    )(live, queries, seg_kv, outgoing)


def solution(mesh):
    in_specs = (
        P(("groups", "nodes"), None),
        P(None, ("groups", "nodes"), None),
        P(None, ("groups", "nodes"), None, None),
        P("groups"),
        P("groups"),
        P("groups", None),
        P("groups", None),
    )
    out_specs = P(("groups", "nodes"), None)
    return jax.shard_map(local, mesh=mesh, in_specs=in_specs, out_specs=out_specs, check_vma=False)
```

```python
import functools
import math

import jax
import jax.numpy as jnp
from jax import lax
from jax.experimental import pallas as pl
from jax.experimental.pallas import tpu as pltpu
from jax.sharding import PartitionSpec as P

HEADS = 16
KV_HEADS = 8
HEAD_DIM = 128
DEPTHS = 4
TEAM = 4

score_scale = 168.0 ** (-0.5)
log2_scale = score_scale * math.log2(math.e)
DEAD = -1e30


def pick_kernel(up_ref, parent_ref, owner_ref, slot_ref, store_ref, out_ref, live_ref, sems):
    me = lax.axis_index("nodes")
    my_segment = me // TEAM
    nodes = live_ref.shape[0]
    segs = out_ref.shape[1]
    pages = owner_ref.shape[0]

    def copies(seg, slot):
        return [
            pltpu.make_async_copy(store_ref.at[half, slot], out_ref.at[half, seg], sems.at[half, seg])
            for half in range(2)
        ]

    def one_segment(seg, carry):
        current = parent_ref[seg]
        slot = jnp.int32(0)
        for _ in range(DEPTHS):
            live = current >= 0
            safe = jnp.maximum(current, 0)

            def one_page(page, slot):
                owner = owner_ref[page, safe]
                hit = jnp.logical_and(live, owner == me)
                return jnp.where(hit, slot_ref[page, safe], slot)

            slot = lax.fori_loop(0, pages, one_page, slot, unroll=pages <= 4)
            current = jnp.where(live, up_ref[safe], -1)
        for copy in copies(seg, slot):
            copy.start()
        return carry

    lax.fori_loop(0, segs, one_segment, 0)

    def clear(node, carry):
        live_ref[node] = jnp.float32(DEAD)
        return carry

    lax.fori_loop(0, nodes, clear, 0)
    current = parent_ref[my_segment]
    for _ in range(DEPTHS):
        live = current >= 0
        safe = jnp.maximum(current, 0)

        @pl.when(live)
        def _():
            def mark(page, carry):
                live_ref[owner_ref[page, safe]] = jnp.float32(0)
                return carry

            lax.fori_loop(0, pages, mark, 0, unroll=pages <= 4)

        current = jnp.where(live, up_ref[safe], -1)

    def finish(seg, carry):
        for copy in copies(seg, 0):
            copy.wait()
        return carry

    lax.fori_loop(0, segs, finish, 0)


def attend_kernel(
    live_ref, q_ref, kv_ref, page_ref, out_ref,
    q_buf, own_buf, anc_buf, acc_ref, max_ref, sum_ref, res_buf,
    q_send, q_recv, kv_send, kv_recv, page_send, page_recv, res_send, res_recv,
):
    me = lax.axis_index("nodes")
    member = me % TEAM
    segment = me // TEAM
    segs = page_ref.shape[1]
    nodes = segs * TEAM
    tok = q_ref.shape[0]
    seg_tok = tok * TEAM
    q_cols = q_buf.shape[2]
    kv_cols = own_buf.shape[3]
    page_tok = page_ref.shape[2]
    heads = q_cols // HEAD_DIM
    group = HEADS // KV_HEADS

    barrier = pltpu.get_barrier_semaphore()

    def greet(step, carry):
        other = lax.rem(me + step, nodes)
        pl.semaphore_signal(barrier, inc=1, device_id={"nodes": other}, device_id_type=pl.DeviceIdType.MESH)
        return carry

    lax.fori_loop(1, nodes, greet, 0)
    pl.semaphore_wait(barrier, nodes - 1)

    def q_copy(step):
        peer = lax.rem(member + step, TEAM)
        return pltpu.make_async_remote_copy(
            src_ref=q_ref.at[:, pl.ds(pl.multiple_of(peer * q_cols, q_cols), q_cols)],
            dst_ref=q_buf.at[member],
            send_sem=q_send.at[peer],
            recv_sem=q_recv.at[member],
            device_id={"nodes": segment * TEAM + peer},
            device_id_type=pl.DeviceIdType.MESH,
        )

    def kv_copy(step):
        peer = lax.rem(member + step, TEAM)
        return pltpu.make_async_remote_copy(
            src_ref=kv_ref.at[:, :, pl.ds(pl.multiple_of(peer * kv_cols, kv_cols), kv_cols)],
            dst_ref=own_buf.at[:, member],
            send_sem=kv_send.at[peer],
            recv_sem=kv_recv.at[member],
            device_id={"nodes": segment * TEAM + peer},
            device_id_type=pl.DeviceIdType.MESH,
        )

    def q_local():
        return pltpu.make_async_copy(
            q_ref.at[:, pl.ds(pl.multiple_of(member * q_cols, q_cols), q_cols)], q_buf.at[member], q_recv.at[member]
        )

    def kv_local():
        return pltpu.make_async_copy(
            kv_ref.at[:, :, pl.ds(pl.multiple_of(member * kv_cols, kv_cols), kv_cols)],
            own_buf.at[:, member],
            kv_recv.at[member],
        )

    def page_part(dest):
        start = lax.rem(dest, TEAM) * kv_cols
        return page_ref.at[:, dest // TEAM, :, pl.ds(pl.multiple_of(start, kv_cols), kv_cols)]

    def page_copy(dest):
        return pltpu.make_async_remote_copy(
            src_ref=page_part(dest),
            dst_ref=anc_buf.at[:, me],
            send_sem=page_send.at[dest],
            recv_sem=page_recv.at[me],
            device_id={"nodes": dest},
            device_id_type=pl.DeviceIdType.MESH,
        )

    def page_local():
        return pltpu.make_async_copy(page_part(me), anc_buf.at[:, me], page_recv.at[me])

    low = segment < segs // 2

    def far_segment(step):
        return jnp.where(low, segs - 1 - step, step)

    for step in range(1, TEAM):
        q_copy(step).start()
        kv_copy(step).start()
    q_local().start()
    kv_local().start()
    page_local().start()

    def send_pages(index, carry):
        seg = far_segment(index // TEAM)
        dest = seg * TEAM + lax.rem(member + index, TEAM)

        @pl.when(dest != me)
        def _():
            page_copy(dest).start()

        return carry

    lax.fori_loop(0, nodes, send_pages, 0)

    for step in range(TEAM):
        peer = lax.rem(member + step, TEAM)
        pltpu.make_async_copy(q_buf.at[peer], q_buf.at[peer], q_recv.at[peer]).wait()
        pltpu.make_async_copy(own_buf.at[:, peer], own_buf.at[:, peer], kv_recv.at[peer]).wait()

    def head_query(head):
        cols = pl.ds(head * HEAD_DIM, HEAD_DIM)
        return q_buf[:, :, cols].reshape(seg_tok, HEAD_DIM)

    def kv_columns(head):
        return pl.ds(head // group * HEAD_DIM, HEAD_DIM)

    def weighted(values, weights):
        return lax.dot_general(
            values, weights.astype(jnp.bfloat16), (((0,), (0,)), ((), ())), preferred_element_type=jnp.float32
        )

    def score(keys, head):
        return lax.dot_general(
            keys, head_query(head), (((1,), (1,)), ((), ())), preferred_element_type=jnp.float32
        )

    def own_head(head):
        cols = kv_columns(head)
        keys = own_buf[0, :, :, cols].reshape(seg_tok, HEAD_DIM)
        values = own_buf[1, :, :, cols].reshape(seg_tok, HEAD_DIM)
        scores = score(keys, head)
        key_at = lax.broadcasted_iota(jnp.int32, scores.shape, 0)
        query_at = lax.broadcasted_iota(jnp.int32, scores.shape, 1)
        scores = jnp.where(key_at <= query_at, scores, DEAD)
        row_max = jnp.max(scores, axis=0, keepdims=True)
        weights = jnp.exp2((scores - row_max) * log2_scale)
        max_ref[head] = row_max
        sum_ref[head] = jnp.sum(weights, axis=0, keepdims=True)
        acc_ref[head] = weighted(values, weights)

    for head in range(heads):
        own_head(head)

    def res_copy(step, half):
        peer = lax.rem(member + step, TEAM)
        columns = q_cols // 2
        return pltpu.make_async_remote_copy(
            src_ref=res_buf.at[half, peer],
            dst_ref=out_ref.at[:, pl.ds(pl.multiple_of(member * q_cols + half * columns, columns), columns)],
            send_sem=res_send.at[half, peer],
            recv_sem=res_recv.at[half, member],
            device_id={"nodes": segment * TEAM + peer},
            device_id_type=pl.DeviceIdType.MESH,
        )

    def res_local(half):
        columns = q_cols // 2
        return pltpu.make_async_copy(
            res_buf.at[half, member],
            out_ref.at[:, pl.ds(pl.multiple_of(member * q_cols + half * columns, columns), columns)],
            res_recv.at[half, member],
        )

    half_heads = heads // 2

    def give(half):
        for place in range(half_heads):
            head = half * half_heads + place
            result = (acc_ref[head] / sum_ref[head]).T.astype(jnp.bfloat16)
            res_buf[half, :, :, place * HEAD_DIM : (place + 1) * HEAD_DIM] = result.reshape(TEAM, tok, HEAD_DIM)
        for step in range(1, TEAM):
            res_copy(step, half).start()
        res_local(half).start()

    def one_step(step, last):
        seg = far_segment(segs - 1 - step)
        first = pl.multiple_of(seg * TEAM, TEAM)
        for part in range(TEAM):
            block = anc_buf.at[:, first + part]
            pltpu.make_async_copy(block, block, page_recv.at[first + part]).wait()
        def one_head(head):
            cols = kv_columns(head)
            keys = anc_buf[0, pl.ds(first, TEAM), :, cols].reshape(TEAM * page_tok, HEAD_DIM)
            values = anc_buf[1, pl.ds(first, TEAM), :, cols].reshape(TEAM * page_tok, HEAD_DIM)
            scores = score(keys, head)
            scores = jnp.concatenate(
                [
                    scores[part * page_tok : (part + 1) * page_tok] + live_ref[first + part]
                    for part in range(TEAM)
                ],
                axis=0,
            )
            old_max = max_ref[head]
            new_max = jnp.maximum(old_max, jnp.max(scores, axis=0, keepdims=True))
            weights = jnp.exp2((scores - new_max) * log2_scale)
            shrink = jnp.exp2((old_max - new_max) * log2_scale)
            max_ref[head] = new_max
            sum_ref[head] = sum_ref[head] * shrink + jnp.sum(weights, axis=0, keepdims=True)
            acc_ref[head] = acc_ref[head] * shrink + weighted(values, weights)

        for head in range(heads):
            one_head(head)
            if last and head % half_heads == half_heads - 1:
                give(head // half_heads)

    def early_step(step, carry):
        one_step(step, False)
        return carry

    lax.fori_loop(0, segs - 1, early_step, 0)
    one_step(segs - 1, True)

    columns = q_cols // 2
    for half in range(2):
        for step in range(TEAM):
            peer = lax.rem(member + step, TEAM)
            place = out_ref.at[:, pl.ds(pl.multiple_of(peer * q_cols + half * columns, columns), columns)]
            pltpu.make_async_copy(place, place, res_recv.at[half, peer]).wait()
        for step in range(1, TEAM):
            res_copy(step, half).wait_send()
    for step in range(1, TEAM):
        q_copy(step).wait_send()
        kv_copy(step).wait_send()

    def drain(step, carry):
        page_copy(lax.rem(me + step, nodes)).wait_send()
        return carry

    lax.fori_loop(1, nodes, drain, 0)


def local(queries, seg_kv, kv_store, seg_parent, block_up, page_owner, page_slot):
    nodes = lax.axis_size("nodes")
    tok, q_width = queries.shape
    kv_width = seg_kv.shape[2]
    page_tok = kv_store.shape[2]
    q_cols = q_width // TEAM
    kv_cols = kv_width // TEAM
    heads = q_cols // HEAD_DIM
    smem = pl.BlockSpec(memory_space=pltpu.SMEM)
    anywhere = pl.BlockSpec(memory_space=pl.ANY)
    outgoing, live = pl.pallas_call(
        pick_kernel,
        out_shape=(
            pltpu.VMEM((2, nodes // TEAM, page_tok, kv_width), kv_store.dtype),
            pltpu.SMEM((nodes,), jnp.float32),
        ),
        in_specs=[smem, smem, smem, smem, pl.BlockSpec(memory_space=pltpu.HBM)],
        out_specs=(pl.BlockSpec(memory_space=pltpu.VMEM), smem),
        scratch_shapes=[pltpu.SemaphoreType.DMA((2, nodes // TEAM))],
        compiler_params=pltpu.CompilerParams(vmem_limit_bytes=52 * 1024 * 1024),
        name="pick_pages",
    )(block_up, seg_parent, page_owner.T, page_slot.T, kv_store)
    dma = pltpu.SemaphoreType.DMA
    return pl.pallas_call(
        attend_kernel,
        out_shape=jax.ShapeDtypeStruct((tok, q_width), jnp.bfloat16),
        in_specs=[smem, anywhere, anywhere, anywhere],
        out_specs=anywhere,
        scratch_shapes=[
            pltpu.VMEM((TEAM, tok, q_cols), jnp.bfloat16),
            pltpu.VMEM((2, TEAM, tok, kv_cols), jnp.bfloat16),
            pltpu.VMEM((2, nodes, page_tok, kv_cols), jnp.bfloat16),
            pltpu.VMEM((heads, HEAD_DIM, TEAM * tok), jnp.float32),
            pltpu.VMEM((heads, 1, TEAM * tok), jnp.float32),
            pltpu.VMEM((heads, 1, TEAM * tok), jnp.float32),
            pltpu.VMEM((2, TEAM, tok, q_cols // 2), jnp.bfloat16),
            dma((TEAM,)), dma((TEAM,)), dma((TEAM,)), dma((TEAM,)),
            dma((nodes,)), dma((nodes,)), dma((2, TEAM)), dma((2, TEAM)),
        ],
        compiler_params=pltpu.CompilerParams(
            collective_id=0, has_side_effects=True, vmem_limit_bytes=40 * 1024 * 1024
        ),
        name="tree_attention",
    )(live, queries, seg_kv, outgoing)


def solution(mesh):
    in_specs = (
        P(("groups", "nodes"), None),
        P(None, ("groups", "nodes"), None),
        P(None, ("groups", "nodes"), None, None),
        P("groups"),
        P("groups"),
        P("groups", None),
        P("groups", None),
    )
    out_specs = P(("groups", "nodes"), None)
    return jax.shard_map(local, mesh=mesh, in_specs=in_specs, out_specs=out_specs, check_vma=False)
```
